128 devices in a mesh: shards: 4 (over y), context: 4 (over z_lo, core), tensor: 8 (over z_hi, x).
Axes of the slice: x: 4, y: 4, z: 4 (z_hi: 2, z_lo: 2; z = z_hi * 2 + z_lo), core: 2. Of those that a mesh axis runs over, the one named last changes fastest.
Arguments:
- block_input: float32 [8, 512, 1024], P('shards', 'context'), may hold values from -6 to 6
- segment_ids: int32 [8, 512], P('shards', 'context'), may hold values from 0 to 2, as said below
- ln1_gain: bfloat16 [2, 1024], P(None, ('shards', 'context')), may hold values from 0.25 to 1.75
- ln1_bias: bfloat16 [2, 1024], P(None, ('shards', 'context')), may hold values from -3 to 3
- qkv_weight: bfloat16 [2, 1024, 3, 1024], P(None, ('shards', 'context'), None, 'tensor'), may hold values from -0.1875 to 0.1875
- qv_bias: bfloat16 [2, 2, 16, 64], P(None, None, 'tensor', ('shards', 'context')), may hold values from -3 to 3
- out_weight: bfloat16 [2, 1024, 1024], P(None, 'tensor', ('shards', 'context')), may hold values from -0.75 to 0.75
- out_bias: bfloat16 [2, 1024], P(None, ('shards', 'context')), may hold values from -2 to 2
- ln2_gain: bfloat16 [2, 1024], P(None, ('shards', 'context')), may hold values from 0.25 to 1.75
- ln2_bias: bfloat16 [2, 1024], P(None, ('shards', 'context')), may hold values from -3 to 3
- fc_weight: bfloat16 [2, 1024, 4096], P(None, ('shards', 'context'), 'tensor'), may hold values from -0.1875 to 0.1875
- fc_bias: bfloat16 [2, 64, 64], P(None, 'tensor', ('shards', 'context')), may hold values from -3 to 3
- proj_weight: bfloat16 [2, 4096, 1024], P(None, 'tensor', ('shards', 'context')), may hold values from -0.09375 to 0.09375
- proj_bias: bfloat16 [2, 1024], P(None, ('shards', 'context')), may hold values from -2 to 2
- cotangent: float32 [8, 512, 1024], P('shards', 'context'), may hold values from -6 to 6
Outputs:
- block_output: float32 [8, 512, 1024], P('shards', 'context')
- grad_input: float32 [8, 512, 1024], P('shards', 'context')
- grad_ln1_gain: float32 [2, 1024], P(None, ('shards', 'context'))
- grad_ln1_bias: float32 [2, 1024], P(None, ('shards', 'context'))
- grad_qkv_weight: float32 [2, 1024, 3, 1024], P(None, ('shards', 'context'), None, 'tensor')
- grad_qv_bias: float32 [2, 2, 16, 64], P(None, None, 'tensor', ('shards', 'context'))
- grad_out_weight: float32 [2, 1024, 1024], P(None, 'tensor', ('shards', 'context'))
- grad_out_bias: float32 [2, 1024], P(None, ('shards', 'context'))
- grad_ln2_gain: float32 [2, 1024], P(None, ('shards', 'context'))
- grad_ln2_bias: float32 [2, 1024], P(None, ('shards', 'context'))
- grad_fc_weight: float32 [2, 1024, 4096], P(None, ('shards', 'context'), 'tensor')
- grad_fc_bias: float32 [2, 64, 64], P(None, 'tensor', ('shards', 'context'))
- grad_proj_weight: float32 [2, 4096, 1024], P(None, 'tensor', ('shards', 'context'))
- grad_proj_bias: float32 [2, 1024], P(None, ('shards', 'context'))
The draws below stay inside these ranges and needn't reach their ends.
Inputs may be any that keep to these rules, and one draw needn't show every extreme that they name: `segment_ids`: document numbers never fall along a sequence, so that each document is a run of positions.
All inputs are finite; a program needn't handle non-finite values.
Results may differ from the reference program's by a relative error of at most 0.025.
Values may be sent and summed in bfloat16 or wider, within the bound.
No kernel may reach another device: no remote copies, remote signals or barrier semaphores. Data moves between devices by JAX's collectives and lax.ppermute only.
A program may use at most 128 MiB of HBM per device.

```python
import jax
import jax.numpy as jnp
from jax import lax

D = 1024
H = 16
FF = 4096
HD = 64
LAYERS = 2
SEQ_LEN = 512
SEQ_DEV = 2
SEQS = 8
LOCAL_LEN = 128


def draw_segment_ids(key, part):
    key = jax.random.fold_in(key, 11)
    key_list = jax.random.split(key, 5)
    positions = jnp.arange(SEQ_LEN, dtype=jnp.int32)
    first_cut = jax.random.randint(key_list[0], (SEQS,), 1, SEQ_LEN)
    second_cut = jax.random.randint(key_list[1], (SEQS,), 1, SEQ_LEN)
    early_cut = jnp.minimum(first_cut, second_cut)
    late_cut = jnp.maximum(first_cut, second_cut)
    span_start = jax.random.randint(key_list[2], (SEQS,), 1, LOCAL_LEN)
    span_end = jax.random.randint(key_list[3], (SEQS,), SEQ_LEN - LOCAL_LEN + 1, SEQ_LEN)
    chosen = jax.random.randint(key_list[4], (SEQS // SEQ_DEV,), 0, SEQ_DEV)
    seq_index = jnp.arange(SEQS, dtype=jnp.int32)
    picked = seq_index % SEQ_DEV == chosen[seq_index // SEQ_DEV]
    cut_one = jnp.where(picked, span_start, early_cut)
    cut_two = jnp.where(picked, span_end, late_cut)
    first_part = (positions[None, :] >= cut_one[:, None]).astype(jnp.int32)
    second_part = (positions[None, :] >= cut_two[:, None]).astype(jnp.int32)
    return first_part + second_part


def with_spikes(array, rng, source, target, shards_of, factor):
    owner, partner = [(jnp.arange(array.shape[axis_at]) // (array.shape[axis_at] // shards_of)).reshape([-1 if axis == axis_at else 1 for axis in range(array.ndim)]) for axis_at in (source, target)]
    chosen = jax.random.permutation(rng, shards_of)[partner]
    strong = (owner == chosen) | (owner == (partner + shards_of // 2) % shards_of)
    return jnp.where(strong, factor * array, array)


def shard_levels(own_key, extent, shards, least, high):
    def one(position, parts):
        draws = jax.random.uniform(jax.random.fold_in(jax.random.fold_in(own_key, 6), position), (parts,), jnp.float32, least / len(shards), high / len(shards))
        return jnp.repeat(jnp.exp(draws), extent[position] // parts).reshape((-1,) + (1,) * (len(extent) - position - 1))

    loudness = one(*shards[0])
    for cut in shards[1:]:
        loudness = loudness * one(*cut)
    return loudness


def bell_draw(key, extent, scale, limit, shards=(), kind=jnp.bfloat16):
    gain = shard_levels(key, extent, shards, -0.22, 0.18) if shards else 1.0
    array = jax.random.normal(key, extent, jnp.float32) * scale * gain
    return jnp.minimum(jnp.maximum(array, -limit), limit).astype(kind)


def noise_with(key, shape, width, limit, cuts, heavy, kind=jnp.bfloat16):
    drawn = width * jax.random.normal(key, shape, jnp.float32)
    if cuts:
        drawn = drawn * shard_levels(key, shape, cuts, -0.22, 0.18)
    return jnp.clip(with_spikes(drawn, jax.random.fold_in(key, 3), *heavy), -limit, limit).astype(kind)


def setup_inputs(seed: int = 0) -> dict:
    splits = jax.random.split(jax.random.key(seed), 16)
    block_input = bell_draw(splits[0], (SEQS, SEQ_LEN, D), 1.0, 6.0, ((0, 4), (1, 4)), jnp.float32)
    segment_ids = draw_segment_ids(jax.random.fold_in(splits[15], 71), 0)
    ln1_gain = jnp.clip(1.0 + 0.15 * jax.random.normal(splits[2], (LAYERS, D), jnp.float32), 0.25, 1.75).astype(jnp.bfloat16)
    ln1_bias = bell_draw(splits[3], (LAYERS, D), 0.5, 3.0, ((1, 16),))
    qkv_weight = bell_draw(splits[4], (LAYERS, D, 3, D), D ** -0.5, 0.1875, ((1, 16), (3, 8)))
    qv_bias = bell_draw(splits[5], (LAYERS, 2, H, HD), 0.5, 3.0, ((2, 8), (3, 16)))
    out_weight = bell_draw(splits[6], (LAYERS, D, D), (D // 16) ** -0.5, 0.75, ((1, 8), (2, 16)))
    out_bias = bell_draw(splits[7], (LAYERS, D), 0.3, 2.0, ((1, 16),))
    ln2_gain = jnp.clip(1.0 + 0.15 * jax.random.normal(splits[8], (LAYERS, D), jnp.float32), 0.25, 1.75).astype(jnp.bfloat16)
    ln2_bias = bell_draw(splits[9], (LAYERS, D), 0.5, 3.0, ((1, 16),))
    fc_weight = bell_draw(splits[10], (LAYERS, D, FF), D ** -0.5, 0.1875, ((1, 16), (2, 8)))
    fc_bias = bell_draw(splits[11], (LAYERS, FF // HD, HD), 0.5, 3.0, ((1, 8), (2, 16)))
    proj_weight = bell_draw(splits[12], (LAYERS, FF, D), FF ** -0.5, 0.09375, ((1, 8), (2, 16)))
    proj_bias = bell_draw(splits[13], (LAYERS, D), 0.3, 2.0, ((1, 16),))
    cotangent = noise_with(splits[14], (SEQS, SEQ_LEN, D), 1.0, 6.0, ((0, 4), (1, 4)), (1, 2, 4, 2.0), jnp.float32)
    return {"block_input": block_input, "segment_ids": segment_ids, "ln1_gain": ln1_gain, "ln1_bias": ln1_bias, "qkv_weight": qkv_weight, "qv_bias": qv_bias, "out_weight": out_weight, "out_bias": out_bias, "ln2_gain": ln2_gain, "ln2_bias": ln2_bias, "fc_weight": fc_weight, "fc_bias": fc_bias, "proj_weight": proj_weight, "proj_bias": proj_bias, "cotangent": cotangent}


epsilon = 1e-05
neg_big = -1e+30
highest = lax.Precision.HIGHEST

@jax.custom_vjp
def low(v):
    return lax.optimization_barrier(v.astype(jnp.bfloat16)).astype(jnp.float32)

@jax.custom_vjp
def low_back(v):
    return v

def low_keep(v):
    return (low(v), None)

def low_pass(kept, grad):
    return (grad,)

def back_keep(v):
    return (v, None)

def back_low(kept, grad):
    return (low(grad),)
low.defvjp(low_keep, low_pass)
low_back.defvjp(back_keep, back_low)

def layer_norm(values, gain_vec, shift_vec):
    centre = values - lax.optimization_barrier(jnp.mean(values, axis=-1, keepdims=True))
    spread = lax.optimization_barrier(jnp.mean(centre * centre, axis=-1, keepdims=True))
    return centre * lax.rsqrt(spread + epsilon) * gain_vec + shift_vec

def attend_sequence(operands):
    queries, key_heads, value_heads, seg_row = operands
    scale_factor = queries.shape[-1] ** (-0.5)
    raw_scores = low_back(jnp.einsum('qhd,khd->hqk', queries, key_heads, precision=highest) * scale_factor)
    positions = jnp.arange(seg_row.shape[0], dtype=jnp.int32)
    allowed = (positions[None, :] <= positions[:, None]) & (seg_row[None, :] == seg_row[:, None])
    masked = jnp.where(allowed[None], raw_scores, neg_big)
    row_max = lax.optimization_barrier(jnp.max(masked, axis=-1, keepdims=True))
    weights_exp = jnp.where(allowed[None], jnp.exp(masked - row_max), 0.0)
    prob = low(weights_exp / lax.optimization_barrier(jnp.sum(weights_exp, axis=-1, keepdims=True)))
    return jnp.einsum('hqk,khd->qhd', prob, value_heads, precision=highest)

def block(residual, seg_ids, weights):
    gain_one, shift_one, qkv_w, qv_bias, out_w, out_bias, gain_two, shift_two, fc_w, fc_bias, proj_w, proj_bias = weights
    seq_count, seq_len, model_width = residual.shape
    flat_in = residual.reshape(-1, model_width)
    normed_one = low(layer_norm(flat_in, gain_one, shift_one))
    projected = jnp.dot(normed_one, qkv_w.reshape(model_width, 3 * model_width), preferred_element_type=jnp.float32, precision=highest)
    projected = projected.reshape(-1, 3, model_width)
    bias_rows = qv_bias.reshape(2, model_width)
    head_count = qv_bias.shape[1]
    shape_heads = (seq_count, seq_len, head_count, model_width // head_count)
    queries = low(low_back(projected[:, 0] + bias_rows[0])).reshape(shape_heads)
    key_heads = low(low_back(projected[:, 1])).reshape(shape_heads)
    value_heads = low(low_back(projected[:, 2] + bias_rows[1])).reshape(shape_heads)
    mixed = lax.map(jax.checkpoint(attend_sequence), (queries, key_heads, value_heads, seg_ids))
    mixed_low = low(low_back(mixed.reshape(-1, model_width)))
    attn_out = low_back(jnp.dot(mixed_low, out_w, preferred_element_type=jnp.float32, precision=highest))
    hidden_one = flat_in + attn_out + out_bias
    normed_two = low(layer_norm(hidden_one, gain_two, shift_two))
    pre_act = low_back(jnp.dot(normed_two, fc_w, preferred_element_type=jnp.float32, precision=highest) + fc_bias.reshape(-1))
    activated = low(jax.nn.gelu(pre_act, approximate=True))
    mlp_out = low_back(jnp.dot(activated, proj_w, preferred_element_type=jnp.float32, precision=highest))
    return (hidden_one + mlp_out + proj_bias).reshape(residual.shape)

def reference(block_input, segment_ids, ln1_gain, ln1_bias, qkv_weight, qv_bias, out_weight, out_bias, ln2_gain, ln2_bias, fc_weight, fc_bias, proj_weight, proj_bias, cotangent):
    params = tuple((member.astype(jnp.float32) for member in (ln1_gain, ln1_bias, qkv_weight, qv_bias, out_weight, out_bias, ln2_gain, ln2_bias, fc_weight, fc_bias, proj_weight, proj_bias)))

    def forward(start, weight_set):
        residual = start
        for layer_at in range(LAYERS):
            residual = block(residual, segment_ids, tuple((member[layer_at] for member in weight_set)))
        return residual
    result, pullback = jax.vjp(forward, block_input.astype(jnp.float32), params)
    grad_start, grad_params = pullback(cotangent.astype(jnp.float32))
    return (result, grad_start, grad_params[0], grad_params[1], grad_params[2], grad_params[3], grad_params[4], grad_params[5], grad_params[6], grad_params[7], grad_params[8], grad_params[9], grad_params[10], grad_params[11])
```

```python
import jax
import jax.numpy as jnp
import numpy as np
from jax import lax
from jax.sharding import Mesh, PartitionSpec as P

EPS = 1e-05
NEG = -1e30
F32 = jnp.float32
BF16 = jnp.bfloat16
OWNERS = ("y", "zl", "c")
PAIR = [(0, 1), (1, 0)]


def mm(left, right, dims):
    return lax.dot_general(left, right, ((dims[0], dims[1]), ((), ())), preferred_element_type=F32)


def nn(left, right):
    return mm(left, right, ((1,), (0,)))


def nt(left, right):
    return mm(left, right, ((1,), (1,)))


def tn(left, right):
    return mm(left, right, ((0,), (0,)))


def core_swap(value):
    return lax.ppermute(value, "c", PAIR)


def zh_swap(value):
    return lax.ppermute(value, "zh", PAIR)


def x_shift(value, step):
    return lax.ppermute(value, "x", [(at, (at + step) % 4) for at in range(4)])


def both_halves(own):
    return jnp.concatenate([own, core_swap(own)], axis=0)


def group_sum(partial_rows):
    half = partial_rows.shape[0] // 2
    got = core_swap(partial_rows[half:].astype(BF16))
    mine = (partial_rows[:half] + got.astype(F32)).astype(BF16)
    right, left, far = x_shift(mine, 1), x_shift(mine, 3), x_shift(mine, 2)
    return (mine.astype(F32) + far.astype(F32)) + (right.astype(F32) + left.astype(F32))


def norm_parts(values):
    centre = values - jnp.mean(values, axis=-1, keepdims=True)
    inv = lax.rsqrt(jnp.mean(centre * centre, axis=-1, keepdims=True) + EPS)
    return centre * inv, inv


def norm(values, gain, shift):
    return norm_parts(values)[0] * gain + shift


def norm_back(values, gain, grad):
    hat, inv = norm_parts(values)
    scaled = grad * gain
    below = inv * (
        scaled
        - jnp.mean(scaled, axis=-1, keepdims=True)
        - hat * jnp.mean(scaled * hat, axis=-1, keepdims=True)
    )
    return below, jnp.sum(grad * hat, axis=0), jnp.sum(grad, axis=0)


def gelu(values):
    return jax.nn.gelu(values, approximate=True)


def heads(rows):
    return rows.reshape(rows.shape[0], 2, 64)


def gather_pack(shard):
    here = lax.axis_index("zh")
    other = zh_swap(shard)
    pair = jnp.where(here == 0, jnp.stack([shard, other]), jnp.stack([other, shard]))
    whole = lax.all_gather(pair, OWNERS, axis=0, tiled=False)
    return lax.dynamic_index_in_dim(whole, lax.axis_index("c"), 1, keepdims=False)


def scatter_pack(grads):
    core = lax.axis_index("c")
    slot = lax.broadcasted_iota(jnp.int32, (1, 2, 1, 1), 1)
    spread = jnp.where(slot == core, grads[:, None], jnp.zeros((), grads.dtype))
    got = lax.psum_scatter(spread, OWNERS, scatter_dimension=0, tiled=False)
    here = lax.axis_index("zh")
    keep = lax.dynamic_index_in_dim(got, here, 0, keepdims=False)
    give = lax.dynamic_index_in_dim(got, 1 - here, 0, keepdims=False)
    return keep.astype(F32) + zh_swap(give).astype(F32)


def per_device(
    block_input, segment_ids, ln1_gain, ln1_bias, qkv_weight, qv_bias, out_weight, out_bias,
    ln2_gain, ln2_bias, fc_weight, fc_bias, proj_weight, proj_bias, cotangent,
):
    core = lax.axis_index("c")
    z_low = lax.axis_index("zl")
    z_high = lax.axis_index("zh")
    layers = 2

    vec_rows = jnp.stack([ln1_gain, ln1_bias, out_bias, ln2_gain, ln2_bias, proj_bias], axis=1)
    vec_rows = vec_rows.reshape(layers, 384)
    small = jnp.concatenate([qv_bias.reshape(-1), fc_bias.reshape(-1)])
    small = jnp.pad(small, (0, 384 - small.shape[0])).reshape(1, 384)
    extra = jnp.pad(jnp.concatenate([vec_rows, small], axis=0), ((0, 13), (0, 0)))
    first = jnp.concatenate([qkv_weight[0].reshape(64, 384), extra], axis=0)

    def mlp_pack(at):
        return [fc_weight[at], proj_weight[at].T, out_weight[at].T]

    pack_a = gather_pack(first)
    pack_b = gather_pack(jnp.concatenate(mlp_pack(0), axis=1)).reshape(1024, 1152)
    pack_c = gather_pack(
        jnp.concatenate(mlp_pack(1) + [qkv_weight[1].reshape(64, 384)], axis=1)
    ).reshape(1024, 1536)

    qkv_ws = [pack_a[:, :64].reshape(1024, 384), pack_c[:, 1152:1536]]
    fc_ws = [pack_b[:, :512], pack_c[:, :512]]
    proj_ws = [pack_b[:, 512:1024], pack_c[:, 512:1024]]
    out_ws = [pack_b[:, 1024:1152], pack_c[:, 1024:1152]]
    vecs = pack_a[:, 64:66].reshape(16, layers, 6, 64).transpose(1, 2, 0, 3)
    vecs = vecs.reshape(layers, 6, 1024).astype(F32)
    smalls = pack_a[:, 66, :96].astype(F32)
    qv_all = smalls[:, :32].reshape(16, layers, 2, 2, 4).transpose(1, 2, 3, 0, 4)
    qv_all = qv_all.reshape(layers, 2, 128)
    fcb_all = smalls[:, 32:96].reshape(16, layers, 8, 4).transpose(1, 2, 0, 3)
    fcb_all = fcb_all.reshape(layers, 512)

    seg = lax.dynamic_index_in_dim(segment_ids, z_high, 0, keepdims=False)
    seg = both_halves(seg)
    seg_prev = lax.ppermute(seg, "zl", [(0, 1)])
    place = jnp.arange(128, dtype=jnp.int32)
    place = jnp.concatenate([core * 128 + place, (1 - core) * 128 + place])
    own_ok = (place[None, :] <= place[:, None]) & (seg[None, :] == seg[:, None])
    prev_ok = (seg_prev[None, :] == seg[:, None]) & (z_low == 1)
    allowed = jnp.concatenate([prev_ok, own_ok], axis=1)[None]

    x = lax.dynamic_index_in_dim(block_input, z_high, 0, keepdims=False)
    states = []
    for at in range(layers):
        g1, b1, ob, g2, b2, pb = [vecs[at, k] for k in range(6)]
        a1 = both_halves(norm(x, g1, b1).astype(BF16))
        proj = nn(a1, qkv_ws[at])
        q = (proj[:, :128] + qv_all[at, 0]).astype(BF16)
        k = proj[:, 128:256].astype(BF16)
        v = (proj[:, 256:] + qv_all[at, 1]).astype(BF16)
        kv = jnp.concatenate([k, v], axis=1)
        kv_all = jnp.concatenate([lax.ppermute(kv, "zl", [(0, 1)]), kv], axis=0)
        k_all, v_all = heads(kv_all[:, :128]), heads(kv_all[:, 128:])
        raw = jnp.einsum("qhd,khd->hqk", heads(q), k_all, preferred_element_type=F32) * 0.125
        masked = jnp.where(allowed, raw, NEG)
        top = jnp.max(masked, axis=-1, keepdims=True)
        e = jnp.where(allowed, jnp.exp(masked - top), 0.0)
        total = jnp.sum(e, axis=-1, keepdims=True)
        p = (e / total).astype(BF16)
        log_total = top + jnp.log(total)
        o = jnp.einsum("hqk,khd->qhd", p, v_all, preferred_element_type=F32)
        o = o.astype(BF16).reshape(256, 128)
        h1 = x + group_sum(nt(o, out_ws[at])) + ob
        a2 = both_halves(norm(h1, g2, b2).astype(BF16))
        u = nn(a2, fc_ws[at]) + fcb_all[at]
        g = gelu(u).astype(BF16)
        y = h1 + group_sum(nt(g, proj_ws[at])) + pb
        states.append((x, a1, q, k_all, v_all, log_total, o, h1, a2, u, g))
        x = y

    def whole_pair(own):
        other = zh_swap(own)
        return jnp.where(z_high == 0, jnp.stack([own, other]), jnp.stack([other, own]))

    block_output = whole_pair(x)

    dy = lax.dynamic_index_in_dim(cotangent, z_high, 0, keepdims=False)
    vec_grads = [None, None]
    qvb_grads = [None, None]
    fcb_grads = [None, None]
    packs = [None, None]
    for at in reversed(range(layers)):
        g1, b1, ob, g2, b2, pb = [vecs[at, k] for k in range(6)]
        x, a1, q, k_all, v_all, log_total, o, h1, a2, u, g = states[at]
        grad_pb = jnp.sum(dy, axis=0)
        dm = both_halves(dy.astype(BF16))
        d_act = nn(dm, proj_ws[at])
        du = jax.vjp(gelu, u)[1](d_act)[0].astype(BF16)
        da2 = group_sum(nt(du, fc_ws[at]))
        grad_proj = tn(dm, g).astype(BF16)
        grad_fc = tn(a2, du).astype(BF16)
        grad_fcb = jnp.sum(du.astype(F32), axis=0)
        below, grad_g2, grad_b2 = norm_back(h1, g2, da2)
        dh1 = dy + below
        grad_ob = jnp.sum(dh1, axis=0)
        da = both_halves(dh1.astype(BF16))
        do = heads(nn(da, out_ws[at]).astype(BF16))
        grad_out = tn(da, o).astype(BF16)
        raw = jnp.einsum("qhd,khd->hqk", heads(q), k_all, preferred_element_type=F32) * 0.125
        p = jnp.where(allowed, jnp.exp(jnp.where(allowed, raw, NEG) - log_total), 0.0)
        dp = jnp.einsum("qhd,khd->hqk", do, v_all, preferred_element_type=F32)
        ds = (p * (dp - jnp.sum(p * dp, axis=-1, keepdims=True))).astype(BF16)
        dq = jnp.einsum("hqk,khd->qhd", ds, k_all, preferred_element_type=F32) * 0.125
        dk = jnp.einsum("hqk,qhd->khd", ds, heads(q), preferred_element_type=F32) * 0.125
        dv = jnp.einsum("hqk,qhd->khd", p.astype(BF16), do, preferred_element_type=F32)
        dkv = jnp.concatenate([dk.reshape(512, 128), dv.reshape(512, 128)], axis=1)
        back = lax.ppermute(dkv[:256].astype(BF16), "zl", [(1, 0)])
        dkv = (dkv[256:] + back.astype(F32)).astype(BF16)
        dqkv = jnp.concatenate([dq.reshape(256, 128).astype(BF16), dkv], axis=1)
        da1 = group_sum(nt(dqkv, qkv_ws[at]))
        grad_qkv = tn(a1, dqkv).astype(BF16)
        qkv_sums = jnp.sum(dqkv.astype(F32), axis=0)
        below, grad_g1, grad_b1 = norm_back(x, g1, da1)
        dy = dh1 + below
        vec_grads[at] = jnp.stack([grad_g1, grad_b1, grad_ob, grad_g2, grad_b2, grad_pb])
        qvb_grads[at] = jnp.stack([qkv_sums[:128], qkv_sums[256:]])
        fcb_grads[at] = grad_fcb
        packs[at] = (grad_fc, grad_proj, grad_out, grad_qkv)

    grad_input = whole_pair(dy.astype(BF16)).astype(F32)

    got_c = scatter_pack(jnp.concatenate(packs[1], axis=1).reshape(16, 64, 1536))
    got_b = scatter_pack(jnp.concatenate(packs[0][:3], axis=1).reshape(16, 64, 1152))

    vec_g = jnp.stack(vec_grads)
    vec_g = vec_g.reshape(layers, 6, 16, 64).transpose(2, 0, 1, 3).reshape(16, layers, 384)
    qv_g = jnp.stack(qvb_grads).reshape(layers, 2, 2, 16, 4).transpose(3, 0, 1, 2, 4)
    fc_g = jnp.stack(fcb_grads).reshape(layers, 8, 16, 4).transpose(2, 0, 1, 3)
    small_g = jnp.concatenate([qv_g.reshape(16, 32), fc_g.reshape(16, 64)], axis=1)
    small_g = jnp.pad(small_g, ((0, 0), (0, 288))).reshape(16, 1, 384)
    extra_g = jnp.pad(jnp.concatenate([vec_g, small_g], axis=1), ((0, 0), (0, 13), (0, 0)))
    last = jnp.concatenate([packs[0][3].reshape(16, 64, 384), extra_g.astype(BF16)], axis=1)
    core_g = lax.axis_index("c")
    slot = lax.broadcasted_iota(jnp.int32, (1, 2, 1, 1), 1)
    spread = jnp.where(slot == core_g, last[:, None], jnp.zeros((), BF16))
    got = lax.psum_scatter(spread, OWNERS, scatter_dimension=0, tiled=False)
    keep = lax.dynamic_index_in_dim(got, z_high, 0, keepdims=False)
    give = lax.dynamic_index_in_dim(got, 1 - z_high, 0, keepdims=False)
    taken = zh_swap(give).astype(F32)
    got_a = keep.astype(F32) + taken
    both = (got[0, 64:66].astype(F32) + got[1, 64:66].astype(F32)).astype(BF16)
    vec_out = both.astype(F32) + zh_swap(both).astype(F32)
    vec_out = vec_out.reshape(layers, 6, 64)

    qkv_out = jnp.stack([got_a[:64], got_c[:, 1152:1536]]).reshape(layers, 64, 3, 128)
    fc_out = jnp.stack([got_b[:, :512], got_c[:, :512]])
    proj_out = jnp.stack([got_b[:, 512:1024].T, got_c[:, 512:1024].T])
    out_out = jnp.stack([got_b[:, 1024:1152].T, got_c[:, 1024:1152].T])
    qvb_out = got_a[66, :32].reshape(layers, 2, 2, 4)
    fcb_out = got_a[66, 32:96].reshape(layers, 8, 4)
    v = [vec_out[:, k] for k in range(6)]
    return (
        block_output, grad_input, v[0], v[1], qkv_out, qvb_out, out_out, v[2],
        v[3], v[4], fc_out, fcb_out, proj_out, v[5],
    )


def solution(mesh):
    fine = Mesh(mesh.devices.reshape(4, 2, 2, 2, 4), ("y", "zl", "c", "zh", "x"))
    context, tensor = ("zl", "c"), ("zh", "x")
    rows = P("y", context, None)
    vec = P(None, OWNERS)
    qkv = P(None, OWNERS, None, tensor)
    qvb = P(None, None, tensor, OWNERS)
    outw = P(None, tensor, OWNERS)
    fcw = P(None, OWNERS, tensor)
    return jax.shard_map(
        per_device,
        mesh=fine,
        in_specs=(
            rows, P("y", context), vec, vec, qkv, qvb, outw, vec, vec, vec, fcw, outw, outw, vec, rows,
        ),
        out_specs=(rows, rows, vec, vec, qkv, qvb, outw, vec, vec, vec, fcw, outw, outw, vec),
        check_vma=False,
    )
```

```python
import jax
import jax.numpy as jnp
from jax import lax
from jax.experimental import pallas as pl
from jax.experimental.pallas import tpu as pltpu
from jax.sharding import Mesh, PartitionSpec as P

EPS = 1e-05
NEG = -1e30
F32 = jnp.float32
BF16 = jnp.bfloat16
OWNERS = ("y", "zl", "c")
PAIR = [(0, 1), (1, 0)]
EVEN = [(0, 1), (1, 0), (2, 3), (3, 2)]
ODD = [(1, 2), (2, 1), (3, 0), (0, 3)]
ROOT = 0.7978845608028654
CUBE = 0.044715


def mm(left, right, dims):
    return lax.dot_general(left, right, ((dims[0], dims[1]), ((), ())), preferred_element_type=F32)


def nn(left, right):
    return mm(left, right, ((1,), (0,)))


def nt(left, right):
    return mm(left, right, ((1,), (1,)))


def tn(left, right):
    return mm(left, right, ((0,), (0,)))


def core_swap(value):
    return lax.ppermute(value, "c", PAIR)


def zh_swap(value):
    return lax.ppermute(value, "zh", PAIR)


def y_shift(value, step):
    return lax.ppermute(value, "y", [(at, (at + step) % 4) for at in range(4)])


def z_shift(value, step):
    flat = lambda z: (z % 2) * 2 + z // 2
    return lax.ppermute(value, ("zl", "zh"), [(flat(z), flat((z + step) % 4)) for z in range(4)])


def z_index():
    return 2 * lax.axis_index("zh") + lax.axis_index("zl")


def pick(stack, at):
    return lax.dynamic_index_in_dim(stack, at, 0, keepdims=False)


def tie(*values):
    return lax.optimization_barrier(values)


def group_sum(own, give):
    mine = (own + core_swap(give).astype(F32)).astype(BF16)
    half = mine.shape[0] // 2
    first, second = mine[:half], mine[half:]
    first = (first.astype(F32) + lax.ppermute(first, "x", EVEN).astype(F32)).astype(BF16)
    second = (second.astype(F32) + lax.ppermute(second, "x", ODD).astype(F32)).astype(BF16)
    return first, lax.ppermute(first, "x", ODD), second, lax.ppermute(second, "x", EVEN)


def gather_pair(shard):
    other = zh_swap(shard)
    here = lax.axis_index("zh")
    pair = jnp.where(here == 0, jnp.stack([shard, other]), jnp.stack([other, shard]))
    return lax.all_gather(pair, OWNERS, axis=0, tiled=False), other


def gather_small(shard):
    y, z, core = lax.axis_index("y"), z_index(), lax.axis_index("c")
    got = jnp.stack([shard] + [y_shift(shard, step) for step in (1, 2, 3)])
    line = jnp.stack([pick(got, (y - at) % 4) for at in range(4)])
    got = jnp.stack([line] + [z_shift(line, step) for step in (1, 2, 3)])
    plane = jnp.stack([pick(got, (z - at) % 4) for at in range(4)])
    came = core_swap(plane)
    return jnp.where(core == 0, jnp.stack([plane, came]), jnp.stack([came, plane]))


def y_scatter(parts):
    return lax.psum_scatter(parts, "y", scatter_dimension=0)


def y_scatter_quick(parts):
    y = lax.axis_index("y")
    one, three, two = [
        y_shift(pick(parts, (y + step) % 4), step).astype(F32) for step in (1, 3, 2)
    ]
    return ((pick(parts, y).astype(F32) + two) + (one + three)).astype(BF16)


def z_scatter(parts):
    core, z = lax.axis_index("c"), z_index()
    keep = jnp.where(core == 0, parts[0], parts[1])
    give = jnp.where(core == 0, parts[1], parts[0])
    came = core_swap(give)
    slots = jnp.where(core == 0, jnp.concatenate([keep, came]), jnp.concatenate([came, keep]))
    return [pick(slots, z)] + [z_shift(pick(slots, (z + step) % 4), step) for step in (1, 3, 2)]


def plane_sum(value):
    for move in (y_shift, z_shift):
        one, three, two = [move(value, step).astype(F32) for step in (1, 3, 2)]
        value = ((value.astype(F32) + two) + (one + three)).astype(BF16)
    return value


def run(kernel, core, dense, weights, outs):
    def whole(shape):
        return pl.BlockSpec(shape, lambda step, at: (0,) * len(shape))

    def part(block):
        return pl.BlockSpec((16, None, 64, 512), lambda step, at: (0, at[0], 0, block))

    def body(core_ref, *refs):
        kernel(core_ref, *refs)

    return pl.pallas_call(
        body,
        grid_spec=pltpu.PrefetchScalarGridSpec(
            num_scalar_prefetch=1,
            grid=(1,),
            in_specs=[whole(v.shape) for v in dense] + [part(b) for _, b in weights],
            out_specs=[whole(shape) for shape, _ in outs],
        ),
        out_shape=[jax.ShapeDtypeStruct(shape, kind) for shape, kind in outs],
        compiler_params=pltpu.CompilerParams(vmem_limit_bytes=48 * 1024 * 1024),
    )(core, *dense, *[w for w, _ in weights])


def flat(ref):
    return ref[...].reshape(1024, 512)


def rows(own, other):
    return jnp.concatenate([own[...], other[...]], axis=0)


def normal(values):
    centre = values - jnp.mean(values, axis=-1, keepdims=True)
    inv = lax.rsqrt(jnp.mean(centre * centre, axis=-1, keepdims=True) + EPS)
    return centre * inv, inv


def total(first, first_came, second, second_came):
    return jnp.concatenate(
        [
            first[...].astype(F32) + first_came[...].astype(F32),
            second[...].astype(F32) + second_came[...].astype(F32),
        ],
        axis=0,
    )


def split(partial_rows, own_ref, give_ref):
    own_ref[...] = partial_rows[:128]
    give_ref[...] = partial_rows[128:].astype(BF16)


def norm_kernel(bias_at, gain_at, with_norm):
    def kernel(core_ref, x, f, fc, s, sc, vecs, y_ref, *a_ref):
        y = x[...] + total(f, fc, s, sc) + vecs[bias_at : bias_at + 1]
        y_ref[...] = y
        if with_norm:
            hat = normal(y)[0]
            scaled = hat * vecs[gain_at : gain_at + 1] + vecs[gain_at + 1 : gain_at + 2]
            a_ref[0][...] = scaled.astype(BF16)

    return kernel


def norm_back_kernel(gain_at):
    def kernel(core_ref, dy, x, f, fc, s, sc, vecs, dx_ref, low_ref, sums_ref):
        grad = total(f, fc, s, sc)
        hat, inv = normal(x[...])
        scaled = grad * vecs[gain_at : gain_at + 1]
        below = inv * (
            scaled
            - jnp.mean(scaled, axis=-1, keepdims=True)
            - hat * jnp.mean(scaled * hat, axis=-1, keepdims=True)
        )
        dx = dy[...] + below
        dx_ref[...] = dx
        low_ref[...] = dx.astype(BF16)
        sums_ref[...] = jnp.concatenate(
            [
                jnp.sum(grad * hat, axis=0, keepdims=True),
                jnp.sum(grad, axis=0, keepdims=True),
                jnp.sum(dx, axis=0, keepdims=True),
                jnp.zeros((5, 1024), F32),
            ],
            axis=0,
        )

    return kernel


def qkv_kernel(core_ref, own, other, bias, w, q_ref, kv_ref):
    proj = nn(rows(own, other), flat(w)[:, :384])
    q_ref[...] = (proj[:, :128] + bias[0:1]).astype(BF16)
    kv_ref[:, :128] = proj[:, 128:256].astype(BF16)
    kv_ref[:, 128:] = (proj[:, 256:] + bias[1:2]).astype(BF16)


def masks(core_ref, seg_col, seg_row, seg_prev):
    core = core_ref[0]

    def place(axis):
        at = lax.broadcasted_iota(jnp.int32, (256, 256), axis) + 128 * core
        return jnp.where(at >= 256, at - 256, at)

    own = (place(1) <= place(0)) & (seg_col[...] == seg_row[...])
    prev = jnp.broadcast_to(seg_col[...], (256, 256)) == seg_prev[...]
    return jnp.concatenate([prev, own], axis=1)


def attn_kernel(core_ref, q, kv, kv_prev, seg_col, seg_row, seg_prev, w, own_ref, give_ref, o_ref, lse_ref):
    allowed = masks(core_ref, seg_col, seg_row, seg_prev)
    kv_all = jnp.concatenate([kv_prev[...], kv[...]], axis=0)
    q_all = q[...]
    outs, logs = [], []
    for head in range(2):
        lanes = slice(64 * head, 64 * head + 64)
        key, value = kv_all[:, lanes], kv_all[:, 128 + 64 * head : 192 + 64 * head]
        score = jnp.where(allowed, nt(q_all[:, lanes], key) * 0.125, NEG)
        top = jnp.max(score, axis=-1, keepdims=True)
        e = jnp.where(allowed, jnp.exp(score - top), 0.0)
        norm = jnp.sum(e, axis=-1, keepdims=True)
        outs.append(nn((e / norm).astype(BF16), value))
        logs.append(jnp.broadcast_to(top + jnp.log(norm), (256, 64)))
    o = jnp.concatenate(outs, axis=1).astype(BF16)
    o_ref[...] = o
    lse_ref[...] = jnp.concatenate(logs, axis=1)
    split(nt(o, flat(w)[:, 384:]), own_ref, give_ref)


def mlp_kernel(core_ref, own, other, bias, w_fc, w_proj, own_ref, give_ref, u_ref, g_ref):
    u = nn(rows(own, other), flat(w_fc)) + bias[...]
    u_ref[...] = u
    g = (0.5 * u * (1.0 + jnp.tanh(ROOT * (u + CUBE * (u * u * u))))).astype(BF16)
    g_ref[...] = g
    split(nt(g, flat(w_proj)), own_ref, give_ref)


def mlp_back_kernel(core_ref, own, other, u_ref, w_fc, w_proj, own_ref, give_ref, du_ref, sum_ref):
    d_act = nn(rows(own, other), flat(w_proj))
    u = u_ref[...]
    wave = jnp.tanh(ROOT * (u + CUBE * (u * u * u)))
    slope = 0.5 * (1.0 + wave) + 0.5 * u * (1.0 - wave * wave) * (ROOT * (1.0 + 3.0 * CUBE * (u * u)))
    du = (d_act * slope).astype(BF16)
    du_ref[...] = du
    sum_ref[...] = jnp.sum(du.astype(F32), axis=0, keepdims=True)
    split(nt(du, flat(w_fc)), own_ref, give_ref)


def attn_back_kernel(
    core_ref, own, other, q, kv, kv_prev, lse, seg_col, seg_row, seg_prev, w, dq_ref, dkv_ref, back_ref
):
    allowed = masks(core_ref, seg_col, seg_row, seg_prev)
    kv_all = jnp.concatenate([kv_prev[...], kv[...]], axis=0)
    do_all = nn(rows(own, other), flat(w)[:, 384:]).astype(BF16)
    q_all = q[...]
    dqs, dks, dvs = [], [], []
    for head in range(2):
        lanes = slice(64 * head, 64 * head + 64)
        key, value = kv_all[:, lanes], kv_all[:, 128 + 64 * head : 192 + 64 * head]
        query, do = q_all[:, lanes], do_all[:, lanes]
        score = jnp.where(allowed, nt(query, key) * 0.125, NEG)
        p = jnp.where(allowed, jnp.exp(score - lse[:, 64 * head : 64 * head + 1]), 0.0)
        dp = nt(do, value)
        ds = (p * (dp - jnp.sum(p * dp, axis=-1, keepdims=True))).astype(BF16)
        dqs.append(nn(ds, key) * 0.125)
        dks.append(tn(ds, query) * 0.125)
        dvs.append(tn(p.astype(BF16), do))
    dq_ref[...] = jnp.concatenate(dqs, axis=1).astype(BF16)
    dkv = jnp.concatenate(dks + dvs, axis=1)
    back_ref[...] = dkv[:256].astype(BF16)
    dkv_ref[...] = dkv[256:]


def qkv_back_kernel(core_ref, dq, dkv, back, w, own_ref, give_ref, dqkv_ref, sums_ref):
    low = (dkv[...] + back[...].astype(F32)).astype(BF16)
    dqkv = jnp.concatenate([dq[...], low], axis=1)
    dqkv_ref[...] = dqkv
    sums_ref[...] = jnp.sum(dqkv.astype(F32), axis=0, keepdims=True)
    split(nt(dqkv, flat(w)[:, :384]), own_ref, give_ref)


def put(out_ref, cols, value):
    value = value.astype(BF16)
    for at in range(16):
        y, low, core = at // 4, at // 2 % 2, at % 2
        out_ref[y, core, low, :, cols] = value[64 * at : 64 * at + 64]


def attn_grads_kernel(core_ref, a1, b1, dqkv, da, db, o, out_ref):
    put(out_ref, slice(0, 384), tn(rows(a1, b1), dqkv[...]))
    put(out_ref, slice(384, 512), tn(rows(da, db), o[...]))


def mlp_grads_kernel(core_ref, a2, b2, du, dm, em, g, out_ref):
    put(out_ref, slice(0, 512), tn(rows(a2, b2), du[...]))
    put(out_ref, slice(512, 1024), tn(rows(dm, em), g[...]))


def final_kernel(core_ref, *refs):
    qkv_ref, out_ref, fc_ref, proj_ref = refs[8:]

    def term(group):
        own, one, three, two = [ref[...].astype(F32) for ref in group]
        return (own + two) + (one + three)

    mlp_1, rest = term(refs[:4]), term(refs[4:8])
    for layer, attn, mlp in ((1, rest[:, :512], mlp_1), (0, rest[:, 512:1024], rest[:, 1024:])):
        qkv_ref[layer] = attn[:, :384]
        out_ref[layer] = attn[:, 384:]
        fc_ref[layer] = mlp[:, :512]
        proj_ref[layer] = mlp[:, 512:]


def per_device(
    block_input, segment_ids, ln1_gain, ln1_bias, qkv_weight, qv_bias, out_weight, out_bias,
    ln2_gain, ln2_bias, fc_weight, fc_bias, proj_weight, proj_bias, cotangent,
):
    core = lax.axis_index("c")
    z_low = lax.axis_index("zl")
    z_high = lax.axis_index("zh")
    layers = 2
    me = core.reshape(1).astype(jnp.int32)

    def pack(at):
        parts = [qkv_weight[at].reshape(64, 384), out_weight[at].T, fc_weight[at], proj_weight[at].T]
        return jnp.concatenate(parts, axis=1)

    w0, other = gather_pair(pack(0))
    shard_1, other = tie(pack(1), other)
    w1, other = gather_pair(shard_1)
    ws = [w0, w1]

    vec_rows = jnp.stack([ln1_gain, ln1_bias, out_bias, ln2_gain, ln2_bias, proj_bias], axis=1)
    small = jnp.concatenate([vec_rows.reshape(-1), qv_bias.reshape(-1), fc_bias.reshape(-1)])
    small = jnp.pad(small, (0, 1024 - small.shape[0])).reshape(8, 128)
    small, other = tie(small, other)
    small = gather_small(small).reshape(2, 4, 4, 1024)
    vecs = small[:, :2, :, :768].reshape(2, 2, 4, 12, 64).transpose(3, 2, 1, 0, 4)
    vecs = vecs.reshape(12, 1024).astype(F32)
    here = lax.dynamic_slice_in_dim(small, 2 * core, 2, 1)[..., 768:864].transpose(2, 1, 0, 3)
    here = here.reshape(16, 96).astype(F32)
    qv_all = here[:, :32].reshape(16, layers, 2, 2, 4).transpose(1, 2, 3, 0, 4)
    qv_all = qv_all.reshape(layers, 2, 128)
    fcb_all = here[:, 32:].reshape(16, layers, 8, 4).transpose(1, 2, 0, 3).reshape(layers, 1, 512)

    seg = lax.dynamic_index_in_dim(segment_ids, z_high, 0, keepdims=False)
    seg = jnp.concatenate([seg, core_swap(seg)])
    seg_prev = jnp.where(z_low == 1, lax.ppermute(seg, "zl", [(0, 1)]), -1)
    segs = [seg.reshape(256, 1), seg.reshape(1, 256), seg_prev.reshape(1, 256)]

    half_f = ((128, 1024), F32)
    half_b = ((128, 1024), BF16)
    low_rows = lambda cols: ((256, cols), BF16)

    x = lax.dynamic_index_in_dim(block_input, z_high, 0, keepdims=False)
    a_own = (normal(x)[0] * vecs[0] + vecs[1]).astype(BF16)
    states = []
    for at in range(layers):
        w = ws[at]
        a1 = (a_own, core_swap(a_own))
        q, kv = run(qkv_kernel, me, [*a1, qv_all[at]], [(w, 0)], [low_rows(128), low_rows(256)])
        kv_prev = lax.ppermute(kv, "zl", [(0, 1)])
        own, give, o, lse = run(
            attn_kernel, me, [q, kv, kv_prev, *segs], [(w, 0)],
            [half_f, half_b, low_rows(128), ((256, 128), F32)],
        )
        h1, b_own = run(
            norm_kernel(6 * at + 2, 6 * at + 3, True), me, [x, *group_sum(own, give), vecs], [],
            [half_f, half_b],
        )
        a2 = (b_own, core_swap(b_own))
        own, give, u, g = run(
            mlp_kernel, me, [*a2, fcb_all[at]], [(w, 1), (w, 2)],
            [half_f, half_b, ((256, 512), F32), low_rows(512)],
        )
        last = at == layers - 1
        y, *a_next = run(
            norm_kernel(6 * at + 5, 6 * at + 6, not last), me, [h1, *group_sum(own, give), vecs], [],
            [half_f] if last else [half_f, half_b],
        )
        states.append((x, a1, q, kv, kv_prev, lse, o, h1, a2, u, g))
        x = y
        a_own = None if last else a_next[0]

    y_out = x
    dy = lax.dynamic_index_in_dim(cotangent, z_high, 0, keepdims=False)
    dy_low = dy.astype(BF16)
    last_bias = jnp.sum(dy, axis=0, keepdims=True)
    sums = {}
    held = []
    for at in reversed(range(layers)):
        w = ws[at]
        x0, a1, q, kv, kv_prev, lse, o, h1, a2, u, g = states[at]
        dm = (dy_low, core_swap(dy_low))
        own, give, du, sums["fc", at] = run(
            mlp_back_kernel, me, [*dm, u], [(w, 1), (w, 2)],
            [half_f, half_b, low_rows(512), ((1, 512), F32)],
        )
        (pack,) = run(mlp_grads_kernel, me, [*a2, du, *dm, g], [], [((4, 2, 2, 64, 1024), BF16)])
        pieces = group_sum(own, give)
        h1, pack = tie(h1, pack)
        mlp_part = y_scatter(pack)
        dh1, dh1_low, sums["two", at] = run(
            norm_back_kernel(6 * at + 3), me, [dy, h1, *pieces, vecs], [],
            [half_f, half_b, ((8, 1024), F32)],
        )
        if at == 0:
            dh1_low, mlp_1 = tie(dh1_low, held[0])
            terms_1 = z_scatter(mlp_1)
        da = (dh1_low, core_swap(dh1_low))
        dq, dkv, back = run(
            attn_back_kernel, me, [*da, q, kv, kv_prev, lse, *segs], [(w, 0)],
            [low_rows(128), ((256, 256), F32), low_rows(256)],
        )
        if at == 1:
            dq, y_other = tie(dq, zh_swap(y_out))
        else:
            dq, *terms_1 = tie(dq, *terms_1)
        back = lax.ppermute(back, "zl", [(1, 0)])
        own, give, dqkv, sums["qkv", at] = run(
            qkv_back_kernel, me, [dq, dkv, back], [(w, 0)],
            [half_f, half_b, low_rows(384), ((1, 384), F32)],
        )
        (pack,) = run(attn_grads_kernel, me, [*a1, dqkv, *da, o], [], [((4, 2, 2, 64, 512), BF16)])
        pieces = group_sum(own, give)
        x0, pack = tie(x0, pack)
        attn_part = (y_scatter if at == 1 else y_scatter_quick)(pack)
        held += [mlp_part, attn_part]
        dy, dy_low, sums["one", at] = run(
            norm_back_kernel(6 * at), me, [dh1, x0, *pieces, vecs], [],
            [half_f, half_b, ((8, 1024), F32)],
        )

    def whole_pair(own, other):
        return jnp.where(z_high == 0, jnp.stack([own, other]), jnp.stack([other, own]))

    block_output = whole_pair(y_out, y_other)
    grad_input = whole_pair(dy_low, zh_swap(dy_low)).astype(F32)

    rest = jnp.concatenate([held[1], held[3], held[2]], axis=-1)
    dy_low, rest = tie(dy_low, rest)
    qkv_out, out_out, fc_out, proj_out = run(
        final_kernel, me, [*terms_1, *z_scatter(rest)], [],
        [((2, 64, 384), F32), ((2, 64, 128), F32), ((2, 64, 512), F32), ((2, 64, 512), F32)],
    )
    qkv_out = qkv_out.reshape(layers, 64, 3, 128)
    out_out, proj_out = out_out.transpose(0, 2, 1), proj_out.transpose(0, 2, 1)

    biases = [sums["one", 1][2:3], last_bias]
    vec_list = []
    for at in range(layers):
        vec_list += [sums["one", at][:2], sums["two", at][2:3], sums["two", at][:2], biases[at]]
    fcb_row = jnp.concatenate([sums["fc", 0], sums["fc", 1]], axis=1)
    qv = [sums["qkv", at][:, cut] for at in range(layers) for cut in (slice(0, 128), slice(256, 384))]
    qvb_row = jnp.pad(jnp.concatenate(qv, axis=1), ((0, 0), (0, 512)))
    small_g = jnp.concatenate(vec_list + [fcb_row, qvb_row], axis=0)
    small_g = plane_sum(small_g.astype(BF16))
    other_g = core_swap(small_g)
    vec_sum = small_g[:12].astype(F32) + other_g[:12].astype(F32)
    owner = 4 * lax.axis_index("y") + 2 * z_low + core
    vec_out = lax.dynamic_slice_in_dim(vec_sum, owner * 64, 64, 1).reshape(layers, 6, 64)
    rows_out = jnp.where(z_high == core, small_g[12:14], other_g[12:14]).astype(F32)
    fcb_out = lax.dynamic_slice_in_dim(rows_out[0].reshape(layers, 8, 64), owner * 4, 4, 2)
    qvb_out = lax.dynamic_slice_in_dim(
        rows_out[1, :512].reshape(layers, 2, 2, 64), owner * 4, 4, 3
    )

    v = [vec_out[:, k] for k in range(6)]
    return (
        block_output, grad_input, v[0], v[1], qkv_out, qvb_out, out_out, v[2],
        v[3], v[4], fc_out, fcb_out, proj_out, v[5],
    )


def solution(mesh):
    fine = Mesh(mesh.devices.reshape(4, 2, 2, 2, 4), ("y", "zl", "c", "zh", "x"))
    context, tensor = ("zl", "c"), ("zh", "x")
    tokens = P("y", context, None)
    vec = P(None, OWNERS)
    qkv = P(None, OWNERS, None, tensor)
    qvb = P(None, None, tensor, OWNERS)
    outw = P(None, tensor, OWNERS)
    fcw = P(None, OWNERS, tensor)
    return jax.shard_map(
        per_device,
        mesh=fine,
        in_specs=(
            tokens, P("y", context), vec, vec, qkv, qvb, outw, vec, vec, vec, fcw, outw, outw, vec,
            tokens,
        ),
        out_specs=(tokens, tokens, vec, vec, qkv, qvb, outw, vec, vec, vec, fcw, outw, outw, vec),
        check_vma=False,
    )
```

```python
import jax
import jax.numpy as jnp
from jax import lax
from jax.experimental import pallas as pl
from jax.experimental.pallas import tpu as pltpu
from jax.sharding import Mesh, PartitionSpec as P

EPS = 1e-05
NEG = -1e30
F32 = jnp.float32
BF16 = jnp.bfloat16
OWNERS = ("y", "zl", "c")
PAIR = [(0, 1), (1, 0)]
EVEN = [(0, 1), (1, 0), (2, 3), (3, 2)]
ODD = [(1, 2), (2, 1), (3, 0), (0, 3)]
ROOT = 0.7978845608028654
CUBE = 0.044715


def mm(left, right, dims):
    return lax.dot_general(left, right, ((dims[0], dims[1]), ((), ())), preferred_element_type=F32)


def nn(left, right):
    return mm(left, right, ((1,), (0,)))


def nt(left, right):
    return mm(left, right, ((1,), (1,)))


def tn(left, right):
    return mm(left, right, ((0,), (0,)))


def core_swap(value):
    return lax.ppermute(value, "c", PAIR)


def zh_swap(value):
    return lax.ppermute(value, "zh", PAIR)


def y_shift(value, step):
    return lax.ppermute(value, "y", [(at, (at + step) % 4) for at in range(4)])


def z_shift(value, step):
    flat = lambda z: (z % 2) * 2 + z // 2
    return lax.ppermute(value, ("zl", "zh"), [(flat(z), flat((z + step) % 4)) for z in range(4)])


def z_index():
    return 2 * lax.axis_index("zh") + lax.axis_index("zl")


def pick(stack, at):
    return lax.dynamic_index_in_dim(stack, at, 0, keepdims=False)


def tie(*values):
    return lax.optimization_barrier(values)


def group_sum(own, give):
    mine = (own + core_swap(give).astype(F32)).astype(BF16)
    half = mine.shape[0] // 2
    first, second = mine[:half], mine[half:]
    first = (first.astype(F32) + lax.ppermute(first, "x", EVEN).astype(F32)).astype(BF16)
    second = (second.astype(F32) + lax.ppermute(second, "x", ODD).astype(F32)).astype(BF16)
    return first, lax.ppermute(first, "x", ODD), second, lax.ppermute(second, "x", EVEN)


def gather_pair(shard):
    other = zh_swap(shard)
    here = lax.axis_index("zh")
    pair = jnp.where(here == 0, jnp.stack([shard, other]), jnp.stack([other, shard]))
    return lax.all_gather(pair, OWNERS, axis=0, tiled=False), other


def gather_small(shard):
    y, z, core = lax.axis_index("y"), z_index(), lax.axis_index("c")
    got = jnp.stack([shard] + [y_shift(shard, step) for step in (1, 2, 3)])
    line = jnp.stack([pick(got, (y - at) % 4) for at in range(4)])
    got = jnp.stack([line] + [z_shift(line, step) for step in (1, 2, 3)])
    plane = jnp.stack([pick(got, (z - at) % 4) for at in range(4)])
    came = core_swap(plane)
    return jnp.where(core == 0, jnp.stack([plane, came]), jnp.stack([came, plane]))


def y_scatter(parts):
    return lax.psum_scatter(parts, "y", scatter_dimension=0)


def fold(move, chunk):
    own = chunk(0).astype(F32)
    one, three, two = [move(chunk(step), step).astype(F32) for step in (1, 3, 2)]
    return (own + two) + (one + three)


def core_scatter(parts):
    core = lax.axis_index("c")
    keep = jnp.where(core == 0, parts[0], parts[1])
    give = jnp.where(core == 0, parts[1], parts[0])
    came = core_swap(give)
    return jnp.where(core == 0, jnp.concatenate([keep, came]), jnp.concatenate([came, keep]))


def z_terms(chunk):
    return [chunk(0)] + [z_shift(chunk(step), step) for step in (1, 3, 2)]


def z_scatter(parts):
    slots, z = core_scatter(parts), z_index()
    return z_terms(lambda step: pick(slots, (z + step) % 4))


def run(kernel, core, dense, weights, outs):
    def whole(shape):
        return pl.BlockSpec(shape, lambda step, at: (0,) * len(shape))

    def part(block):
        return pl.BlockSpec((16, None, 64, 512), lambda step, at: (0, at[0], 0, block))

    def body(core_ref, *refs):
        kernel(core_ref, *refs)

    return pl.pallas_call(
        body,
        grid_spec=pltpu.PrefetchScalarGridSpec(
            num_scalar_prefetch=1,
            grid=(1,),
            in_specs=[whole(v.shape) for v in dense] + [part(b) for _, b in weights],
            out_specs=[whole(shape) for shape, _ in outs],
        ),
        out_shape=[jax.ShapeDtypeStruct(shape, kind) for shape, kind in outs],
        compiler_params=pltpu.CompilerParams(vmem_limit_bytes=48 * 1024 * 1024),
    )(core, *dense, *[w for w, _ in weights])


def flat(ref):
    return ref[...].reshape(1024, 512)


def rows(own, other):
    return jnp.concatenate([own[...], other[...]], axis=0)


def normal(values):
    centre = values - jnp.mean(values, axis=-1, keepdims=True)
    inv = lax.rsqrt(jnp.mean(centre * centre, axis=-1, keepdims=True) + EPS)
    return centre * inv, inv


def total(first, first_came, second, second_came):
    return jnp.concatenate(
        [
            first[...].astype(F32) + first_came[...].astype(F32),
            second[...].astype(F32) + second_came[...].astype(F32),
        ],
        axis=0,
    )


def split(partial_rows, own_ref, give_ref):
    own_ref[...] = partial_rows[:128]
    give_ref[...] = partial_rows[128:].astype(BF16)


def norm_kernel(bias_at, gain_at, with_norm):
    def kernel(core_ref, x, f, fc, s, sc, vecs, y_ref, *a_ref):
        y = x[...] + total(f, fc, s, sc) + vecs[bias_at : bias_at + 1]
        y_ref[...] = y
        if with_norm:
            hat = normal(y)[0]
            scaled = hat * vecs[gain_at : gain_at + 1] + vecs[gain_at + 1 : gain_at + 2]
            a_ref[0][...] = scaled.astype(BF16)

    return kernel


def norm_back_kernel(gain_at):
    def kernel(core_ref, dy, x, f, fc, s, sc, vecs, dx_ref, low_ref, sums_ref):
        grad = total(f, fc, s, sc)
        hat, inv = normal(x[...])
        scaled = grad * vecs[gain_at : gain_at + 1]
        below = inv * (
            scaled
            - jnp.mean(scaled, axis=-1, keepdims=True)
            - hat * jnp.mean(scaled * hat, axis=-1, keepdims=True)
        )
        dx = dy[...] + below
        dx_ref[...] = dx
        low_ref[...] = dx.astype(BF16)
        sums_ref[...] = jnp.concatenate(
            [
                jnp.sum(grad * hat, axis=0, keepdims=True),
                jnp.sum(grad, axis=0, keepdims=True),
                jnp.sum(dx, axis=0, keepdims=True),
                jnp.zeros((5, 1024), F32),
            ],
            axis=0,
        )

    return kernel


def qkv_kernel(core_ref, own, other, bias, w, q_ref, kv_ref):
    proj = nn(rows(own, other), flat(w)[:, :384])
    q_ref[...] = (proj[:, :128] + bias[0:1]).astype(BF16)
    kv_ref[:, :128] = proj[:, 128:256].astype(BF16)
    kv_ref[:, 128:] = (proj[:, 256:] + bias[1:2]).astype(BF16)


def masks(core_ref, seg_col, seg_row, seg_prev):
    core = core_ref[0]

    def place(axis):
        at = lax.broadcasted_iota(jnp.int32, (256, 256), axis) + 128 * core
        return jnp.where(at >= 256, at - 256, at)

    own = (place(1) <= place(0)) & (seg_col[...] == seg_row[...])
    prev = jnp.broadcast_to(seg_col[...], (256, 256)) == seg_prev[...]
    return jnp.concatenate([prev, own], axis=1)


def attn_kernel(core_ref, q, kv, kv_prev, seg_col, seg_row, seg_prev, w, own_ref, give_ref, o_ref, lse_ref):
    allowed = masks(core_ref, seg_col, seg_row, seg_prev)
    kv_all = jnp.concatenate([kv_prev[...], kv[...]], axis=0)
    q_all = q[...]
    outs, logs = [], []
    for head in range(2):
        lanes = slice(64 * head, 64 * head + 64)
        key, value = kv_all[:, lanes], kv_all[:, 128 + 64 * head : 192 + 64 * head]
        score = jnp.where(allowed, nt(q_all[:, lanes], key) * 0.125, NEG)
        top = jnp.max(score, axis=-1, keepdims=True)
        e = jnp.where(allowed, jnp.exp(score - top), 0.0)
        norm = jnp.sum(e, axis=-1, keepdims=True)
        outs.append(nn((e / norm).astype(BF16), value))
        logs.append(jnp.broadcast_to(top + jnp.log(norm), (256, 64)))
    o = jnp.concatenate(outs, axis=1).astype(BF16)
    o_ref[...] = o
    lse_ref[...] = jnp.concatenate(logs, axis=1)
    split(nt(o, flat(w)[:, 384:]), own_ref, give_ref)


def mlp_kernel(core_ref, own, other, bias, w_fc, w_proj, own_ref, give_ref, u_ref, g_ref):
    u = nn(rows(own, other), flat(w_fc)) + bias[...]
    u_ref[...] = u
    g = (0.5 * u * (1.0 + jnp.tanh(ROOT * (u + CUBE * (u * u * u))))).astype(BF16)
    g_ref[...] = g
    split(nt(g, flat(w_proj)), own_ref, give_ref)


def mlp_back_kernel(core_ref, own, other, u_ref, w_fc, w_proj, own_ref, give_ref, du_ref, sum_ref):
    d_act = nn(rows(own, other), flat(w_proj))
    u = u_ref[...]
    wave = jnp.tanh(ROOT * (u + CUBE * (u * u * u)))
    slope = 0.5 * (1.0 + wave) + 0.5 * u * (1.0 - wave * wave) * (ROOT * (1.0 + 3.0 * CUBE * (u * u)))
    du = (d_act * slope).astype(BF16)
    du_ref[...] = du
    sum_ref[...] = jnp.sum(du.astype(F32), axis=0, keepdims=True)
    split(nt(du, flat(w_fc)), own_ref, give_ref)


def attn_back_kernel(
    core_ref, own, other, q, kv, kv_prev, lse, seg_col, seg_row, seg_prev, w, dq_ref, dkv_ref, back_ref
):
    allowed = masks(core_ref, seg_col, seg_row, seg_prev)
    kv_all = jnp.concatenate([kv_prev[...], kv[...]], axis=0)
    do_all = nn(rows(own, other), flat(w)[:, 384:]).astype(BF16)
    q_all = q[...]
    dqs, dks, dvs = [], [], []
    for head in range(2):
        lanes = slice(64 * head, 64 * head + 64)
        key, value = kv_all[:, lanes], kv_all[:, 128 + 64 * head : 192 + 64 * head]
        query, do = q_all[:, lanes], do_all[:, lanes]
        score = jnp.where(allowed, nt(query, key) * 0.125, NEG)
        p = jnp.where(allowed, jnp.exp(score - lse[:, 64 * head : 64 * head + 1]), 0.0)
        dp = nt(do, value)
        ds = (p * (dp - jnp.sum(p * dp, axis=-1, keepdims=True))).astype(BF16)
        dqs.append(nn(ds, key) * 0.125)
        dks.append(tn(ds, query) * 0.125)
        dvs.append(tn(p.astype(BF16), do))
    dq_ref[...] = jnp.concatenate(dqs, axis=1).astype(BF16)
    dkv = jnp.concatenate(dks + dvs, axis=1)
    back_ref[...] = dkv[:256].astype(BF16)
    dkv_ref[...] = dkv[256:]


def qkv_back_kernel(core_ref, dq, dkv, back, w, own_ref, give_ref, dqkv_ref, sums_ref):
    low = (dkv[...] + back[...].astype(F32)).astype(BF16)
    dqkv = jnp.concatenate([dq[...], low], axis=1)
    dqkv_ref[...] = dqkv
    sums_ref[...] = jnp.sum(dqkv.astype(F32), axis=0, keepdims=True)
    split(nt(dqkv, flat(w)[:, :384]), own_ref, give_ref)


def put(out_ref, cols, value):
    value = value.astype(BF16)
    for at in range(16):
        y, low, core = at // 4, at // 2 % 2, at % 2
        out_ref[y, core, low, :, cols] = value[64 * at : 64 * at + 64]


def attn_grads_kernel(core_ref, a1, b1, dqkv, da, db, o, out_ref):
    put(out_ref, slice(0, 384), tn(rows(a1, b1), dqkv[...]))
    put(out_ref, slice(384, 512), tn(rows(da, db), o[...]))


def mlp_grads_kernel(core_ref, a2, b2, du, dm, em, g, out_ref):
    put(out_ref, slice(0, 512), tn(rows(a2, b2), du[...]))
    put(out_ref, slice(512, 1024), tn(rows(dm, em), g[...]))


def final_kernel(core_ref, *refs):
    qkv_ref, out_ref, fc_ref, proj_ref, vec_ref = refs[12:]

    def term(group):
        own, one, three, two = [ref[...].astype(F32) for ref in group]
        return (own + two) + (one + three)

    mlp_1, middle, last = [term(refs[at : at + 4]) for at in (0, 4, 8)]
    vec_ref[...] = last[64:]
    for layer, attn, mlp in ((1, middle[:, :512], mlp_1), (0, last[:64], middle[:, 512:])):
        qkv_ref[layer] = attn[:, :384]
        out_ref[layer] = attn[:, 384:]
        fc_ref[layer] = mlp[:, :512]
        proj_ref[layer] = mlp[:, 512:]


def per_device(
    block_input, segment_ids, ln1_gain, ln1_bias, qkv_weight, qv_bias, out_weight, out_bias,
    ln2_gain, ln2_bias, fc_weight, fc_bias, proj_weight, proj_bias, cotangent,
):
    core = lax.axis_index("c")
    z_low = lax.axis_index("zl")
    z_high = lax.axis_index("zh")
    layers = 2
    me = core.reshape(1).astype(jnp.int32)

    def pack(at):
        parts = [qkv_weight[at].reshape(64, 384), out_weight[at].T, fc_weight[at], proj_weight[at].T]
        return jnp.concatenate(parts, axis=1)

    w0, other = gather_pair(pack(0))
    shard_1, other = tie(pack(1), other)
    w1, other = gather_pair(shard_1)
    ws = [w0, w1]

    vec_rows = jnp.stack([ln1_gain, ln1_bias, out_bias, ln2_gain, ln2_bias, proj_bias], axis=1)
    small = jnp.concatenate([vec_rows.reshape(-1), qv_bias.reshape(-1), fc_bias.reshape(-1)])
    small = jnp.pad(small, (0, 1024 - small.shape[0])).reshape(8, 128)
    small, other = tie(small, other)
    small = gather_small(small).reshape(2, 4, 4, 1024)
    vecs = small[:, :2, :, :768].reshape(2, 2, 4, 12, 64).transpose(3, 2, 1, 0, 4)
    vecs = vecs.reshape(12, 1024).astype(F32)
    here = lax.dynamic_slice_in_dim(small, 2 * core, 2, 1)[..., 768:864].transpose(2, 1, 0, 3)
    here = here.reshape(16, 96).astype(F32)
    qv_all = here[:, :32].reshape(16, layers, 2, 2, 4).transpose(1, 2, 3, 0, 4)
    qv_all = qv_all.reshape(layers, 2, 128)
    fcb_all = here[:, 32:].reshape(16, layers, 8, 4).transpose(1, 2, 0, 3).reshape(layers, 1, 512)

    seg = lax.dynamic_index_in_dim(segment_ids, z_high, 0, keepdims=False)
    seg = jnp.concatenate([seg, core_swap(seg)])
    seg_prev = jnp.where(z_low == 1, lax.ppermute(seg, "zl", [(0, 1)]), -1)
    segs = [seg.reshape(256, 1), seg.reshape(1, 256), seg_prev.reshape(1, 256)]

    half_f = ((128, 1024), F32)
    half_b = ((128, 1024), BF16)
    low_rows = lambda cols: ((256, cols), BF16)

    x = lax.dynamic_index_in_dim(block_input, z_high, 0, keepdims=False)
    a_own = (normal(x)[0] * vecs[0] + vecs[1]).astype(BF16)
    states = []
    for at in range(layers):
        w = ws[at]
        a1 = (a_own, core_swap(a_own))
        q, kv = run(qkv_kernel, me, [*a1, qv_all[at]], [(w, 0)], [low_rows(128), low_rows(256)])
        kv_prev = lax.ppermute(kv, "zl", [(0, 1)])
        own, give, o, lse = run(
            attn_kernel, me, [q, kv, kv_prev, *segs], [(w, 0)],
            [half_f, half_b, low_rows(128), ((256, 128), F32)],
        )
        h1, b_own = run(
            norm_kernel(6 * at + 2, 6 * at + 3, True), me, [x, *group_sum(own, give), vecs], [],
            [half_f, half_b],
        )
        a2 = (b_own, core_swap(b_own))
        own, give, u, g = run(
            mlp_kernel, me, [*a2, fcb_all[at]], [(w, 1), (w, 2)],
            [half_f, half_b, ((256, 512), F32), low_rows(512)],
        )
        last = at == layers - 1
        y, *a_next = run(
            norm_kernel(6 * at + 5, 6 * at + 6, not last), me, [h1, *group_sum(own, give), vecs], [],
            [half_f] if last else [half_f, half_b],
        )
        states.append((x, a1, q, kv, kv_prev, lse, o, h1, a2, u, g))
        x = y
        a_own = None if last else a_next[0]

    y_out = x

    def whole_pair(own, other):
        return jnp.where(z_high == 0, jnp.stack([own, other]), jnp.stack([other, own]))

    dy = lax.dynamic_index_in_dim(cotangent, z_high, 0, keepdims=False)
    dy_low = dy.astype(BF16)
    last_bias = jnp.sum(dy, axis=0, keepdims=True)
    sums = {}
    held = []
    for at in reversed(range(layers)):
        w = ws[at]
        x0, a1, q, kv, kv_prev, lse, o, h1, a2, u, g = states[at]
        dm = (dy_low, core_swap(dy_low))
        own, give, du, sums["fc", at] = run(
            mlp_back_kernel, me, [*dm, u], [(w, 1), (w, 2)],
            [half_f, half_b, low_rows(512), ((1, 512), F32)],
        )
        (pack,) = run(mlp_grads_kernel, me, [*a2, du, *dm, g], [], [((4, 2, 2, 64, 1024), BF16)])
        pieces = group_sum(own, give)
        h1, pack = tie(h1, pack)
        mlp_part = y_scatter(pack)
        dh1, dh1_low, sums["two", at] = run(
            norm_back_kernel(6 * at + 3), me, [dy, h1, *pieces, vecs], [],
            [half_f, half_b, ((8, 1024), F32)],
        )
        if at == 0:
            dh1_low, mlp_1 = tie(dh1_low, held[0])
            terms_1 = z_scatter(mlp_1)
        da = (dh1_low, core_swap(dh1_low))
        dq, dkv, back = run(
            attn_back_kernel, me, [*da, q, kv, kv_prev, lse, *segs], [(w, 0)],
            [low_rows(128), ((256, 256), F32), low_rows(256)],
        )
        if at == 1:
            dq, block_output = tie(dq, whole_pair(y_out, zh_swap(y_out)))
        else:
            dq, *terms_1 = tie(dq, *terms_1)
        back = lax.ppermute(back, "zl", [(1, 0)])
        own, give, dqkv, sums["qkv", at] = run(
            qkv_back_kernel, me, [dq, dkv, back], [(w, 0)],
            [half_f, half_b, low_rows(384), ((1, 384), F32)],
        )
        (pack,) = run(attn_grads_kernel, me, [*a1, dqkv, *da, o], [], [((4, 2, 2, 64, 512), BF16)])
        pieces = group_sum(own, give)
        x0, pack = tie(x0, pack)
        held += [mlp_part, y_scatter(pack) if at == 1 else pack]
        dy, dy_low, sums["one", at] = run(
            norm_back_kernel(6 * at), me, [dh1, x0, *pieces, vecs], [],
            [half_f, half_b, ((8, 1024), F32)],
        )

    grad_input = whole_pair(dy_low, zh_swap(dy_low)).astype(F32)

    biases = [sums["one", 1][2:3], last_bias]
    vec_list = []
    for at in range(layers):
        vec_list += [sums["one", at][:2], sums["two", at][2:3], sums["two", at][:2], biases[at]]
    fcb_row = jnp.concatenate([sums["fc", 0], sums["fc", 1]], axis=1)
    qv = [sums["qkv", at][:, cut] for at in range(layers) for cut in (slice(0, 128), slice(256, 384))]
    qvb_row = jnp.pad(jnp.concatenate(qv, axis=1), ((0, 0), (0, 512)))
    small_g = jnp.concatenate(vec_list + [fcb_row, qvb_row], axis=0)
    small_g = jnp.pad(small_g.astype(BF16), ((0, 2), (0, 0))).reshape(32, 512)

    middle = jnp.concatenate([held[1], held[2]], axis=-1)
    dy_low, middle = tie(dy_low, middle)
    middle = z_scatter(middle)

    y, z = lax.axis_index("y"), z_index()
    pack = held[3].reshape(4, 256, 512)
    line = fold(
        y_shift, lambda step: jnp.concatenate([pick(pack, (y + step) % 4), small_g], axis=0)
    ).astype(BF16)
    line, *middle = tie(line, *middle)
    slots = core_scatter(line[:256].reshape(2, 2, 64, 512))
    small_g = line[256:].reshape(16, 1024)
    other_g = core_swap(small_g)
    vec_sum = (small_g[:12].astype(F32) + other_g[:12].astype(F32)).astype(BF16)

    def chunk(step):
        place = (z + step) % 4
        biases = jnp.where(place // 2 == core, small_g[12:], other_g[12:])
        extra = jnp.concatenate([vec_sum, biases], axis=0)
        return jnp.concatenate([pick(slots, place), extra.reshape(32, 512)], axis=0)

    qkv_out, out_out, fc_out, proj_out, small_out = run(
        final_kernel, me, [*terms_1, *middle, *z_terms(chunk)], [],
        [
            ((2, 64, 384), F32), ((2, 64, 128), F32), ((2, 64, 512), F32), ((2, 64, 512), F32),
            ((32, 512), F32),
        ],
    )
    qkv_out = qkv_out.reshape(layers, 64, 3, 128)
    out_out, proj_out = out_out.transpose(0, 2, 1), proj_out.transpose(0, 2, 1)
    small_out = small_out.reshape(16, 1024)
    owner = 4 * y + 2 * z_low + core
    vec_out = lax.dynamic_slice_in_dim(small_out[:12], owner * 64, 64, 1).reshape(layers, 6, 64)
    fcb_out = lax.dynamic_slice_in_dim(small_out[12].reshape(layers, 8, 64), owner * 4, 4, 2)
    qvb_out = lax.dynamic_slice_in_dim(
        small_out[13, :512].reshape(layers, 2, 2, 64), owner * 4, 4, 3
    )
    v = [vec_out[:, k] for k in range(6)]
    return (
        block_output, grad_input, v[0], v[1], qkv_out, qvb_out, out_out, v[2],
        v[3], v[4], fc_out, fcb_out, proj_out, v[5],
    )


def solution(mesh):
    fine = Mesh(mesh.devices.reshape(4, 2, 2, 2, 4), ("y", "zl", "c", "zh", "x"))
    context, tensor = ("zl", "c"), ("zh", "x")
    tokens = P("y", context, None)
    vec = P(None, OWNERS)
    qkv = P(None, OWNERS, None, tensor)
    qvb = P(None, None, tensor, OWNERS)
    outw = P(None, tensor, OWNERS)
    fcw = P(None, OWNERS, tensor)
    return jax.shard_map(
        per_device,
        mesh=fine,
        in_specs=(
            tokens, P("y", context), vec, vec, qkv, qvb, outw, vec, vec, vec, fcw, outw, outw, vec,
            tokens,
        ),
        out_specs=(tokens, tokens, vec, vec, qkv, qvb, outw, vec, vec, vec, fcw, outw, outw, vec),
        check_vma=False,
    )
```
